128 devices in a mesh: chan: 32 (over z, y, core), grp: 4 (over x).
Axes of the slice: x: 4, y: 4, z: 4, core: 2. Of those that a mesh axis runs over, the one named last changes fastest.
Arguments:
- beam_power: bfloat16 [128, 8192, 128], P('grp', 'chan'), as said below
- trial_blocks: int32 [128], replicated, may hold values from 1 to 4, as said below
- shift_table: int32 [4, 5, 8192], replicated, may hold values from 0 to 4, as said below
Outputs:
- dm_planes: bfloat16 [128, 4, 8192, 128], P(('grp', 'chan'))
The draws below stay inside these ranges and needn't reach their ends.
Inputs may be any that keep to these rules, and one draw needn't show every extreme that they name: `beam_power`: detected power, drawn afresh for every beam, channel and sample. `trial_blocks`: DM blocks needed by each beam. `shift_table`: delays in whole tiles.
All inputs are finite; a program needn't handle non-finite values.
Results may differ from the reference program's by a relative error of at most 0.0049.
Values may be sent and summed in bfloat16 or wider, within the bound.
No kernel may reach another device: no remote copies, remote signals or barrier semaphores. Data moves between devices by JAX's collectives and lax.ppermute only.
A program may use at most 128 MiB of HBM per device.

```python
import math
import jax
import jax.numpy as jnp
from jax import lax

NCHAN = 8192
NT = 128
SECTIONS = 5
MAXBLK = 4
TILE = 8
BEAMS = 128
MAXSH = 4


def draw_beam_power(key, part):
    key = jax.random.fold_in(key, 5)
    keys_list = jax.random.split(key, 4)
    chan_gain = jnp.exp(jax.random.uniform(keys_list[0], (NCHAN,), jnp.float32, 0.0, math.log(10.0)))
    beam_gain = jnp.exp(jax.random.uniform(keys_list[1], (BEAMS,), jnp.float32, 0.0, math.log(10.0)))
    level_base = jax.random.uniform(keys_list[2], (BEAMS, NCHAN, 1), jnp.float32, 2.0, 6.0)
    noise_part = jax.random.normal(keys_list[3], (BEAMS, NCHAN, NT), jnp.float32)
    values = beam_gain[:, None, None] * chan_gain[None, :, None] * (level_base + noise_part)
    return values.astype(jnp.bfloat16)


def draw_trial_blocks(key, part):
    key = jax.random.fold_in(key, 11)
    keys_list = jax.random.split(key, 3)
    raw_draw = jax.random.randint(keys_list[0], (BEAMS,), 0, 16)
    counts_out = 1 + (raw_draw >= 8).astype(jnp.int32) + (raw_draw >= 12).astype(jnp.int32) + (raw_draw >= 14).astype(jnp.int32)
    high_place = jax.random.randint(keys_list[1], (), 0, BEAMS)
    counts_out = counts_out.at[high_place].set(MAXBLK)
    low_place = (high_place + 1 + jax.random.randint(keys_list[2], (), 0, BEAMS - 1)) % BEAMS
    counts_out = counts_out.at[low_place].set(1)
    return counts_out.astype(jnp.int32)


def draw_shift_table(key, part):
    key = jax.random.fold_in(key, 17)
    table_out = jax.random.randint(key, (MAXBLK, SECTIONS, NCHAN), 0, MAXSH + 1)
    table_out = table_out.at[0, 0, 0].set(MAXSH)
    table_out = table_out.at[MAXBLK - 1, SECTIONS - 1, NCHAN - 1].set(0)
    return table_out.astype(jnp.int32)


def setup_inputs(seed: int = 0) -> dict:
    streams_of = jax.random.split(jax.random.key(seed), 4)
    return {
        "beam_power": draw_beam_power(jax.random.fold_in(streams_of[3], 71), 0),
        "trial_blocks": draw_trial_blocks(jax.random.fold_in(streams_of[3], 71), 0),
        "shift_table": draw_shift_table(jax.random.fold_in(streams_of[3], 71), 0),
    }


epsilon = 1e-05

def normalize(block_power):
    values = block_power.astype(jnp.float32)
    center = lax.optimization_barrier(jnp.mean(values, axis=-1, keepdims=True))
    spread = lax.optimization_barrier(jnp.mean(jnp.square(values - center), axis=-1, keepdims=True))
    return ((values - center) * lax.rsqrt(spread + epsilon)).astype(jnp.bfloat16)

def shift_tiles(block_rows, amount):
    band_count, group_size, time_len = block_rows.shape
    tile_count = time_len // TILE
    tiled = block_rows.reshape(band_count, group_size, tile_count, TILE)
    source_tile = jnp.arange(tile_count, dtype=jnp.int32)[None, None, :] - amount[:, :, None]
    picked = jnp.take_along_axis(tiled, jnp.maximum(source_tile, 0)[..., None], axis=2)
    result = jnp.where((source_tile >= 0)[..., None], picked, 0.0)
    return result.reshape(band_count, group_size, time_len)

def dedisperse(rows_in, section_shifts):
    row_count, time_len = rows_in.shape
    current = rows_in
    for level_index in range(section_shifts.shape[0]):
        half_size = 2 ** level_index
        group_size = 2 * half_size
        grouped = current.reshape(row_count // group_size, 2, half_size, time_len)
        lower_band = grouped[:, 0]
        upper_band = grouped[:, 1]
        low_rows = jnp.repeat(lower_band, 2, axis=1)
        if half_size == 1:
            high_rows = jnp.repeat(upper_band, 2, axis=1)
        else:
            high_rows = jnp.concatenate([upper_band[:, :1], jnp.repeat(upper_band[:, 1:], 2, axis=1), upper_band[:, -1:]], axis=1)
        moved_rows = shift_tiles(high_rows, section_shifts[level_index].reshape(row_count // group_size, group_size))
        current = (low_rows + moved_rows).reshape(row_count, time_len)
    return current

def reference(beam_power, trial_blocks, shift_table):
    out_scale = float(2 ** SECTIONS) ** (-0.5)

    def per_beam(inputs):
        one_power, one_count = inputs
        calibrated = normalize(one_power).astype(jnp.float32)
        planes_list = []
        for block_index in range(MAXBLK):
            time_plane = dedisperse(calibrated, shift_table[block_index]) * out_scale
            planes_list.append(jnp.where(block_index < one_count, time_plane, 0.0).astype(jnp.bfloat16))
        return jnp.stack(planes_list)
    return lax.map(per_beam, (beam_power, trial_blocks))
```

```python
import jax
import jax.numpy as jnp
from jax import lax
from jax.experimental import pallas as pl
from jax.experimental.pallas import tpu as pltpu
from jax.sharding import PartitionSpec as P

SECTIONS = 5
MAXBLK = 4
TILE = 8
BAND = 32
LANES = 128
EPS = 1e-05


def delayed(rows, tiles):
    pad = jnp.zeros((tiles,) + rows.shape[1:], rows.dtype)
    return jnp.concatenate([pad, rows[:-tiles]], axis=0)


def delay_rows(rows, amount):
    out = rows
    for bit in range(3):
        out = jnp.where((amount & (1 << bit)) != 0, delayed(out, 1 << bit), out)
    return out


def kernel(counts, raw, table, out, start, ping, pong, turn):
    block = pl.program_id(1)
    tiles = 128 // TILE
    scale = float(2**SECTIONS) ** (-0.5)

    @pl.when(block == 0)
    def _():
        turn[...] = raw[...].reshape(turn.shape).astype(jnp.float32)

        def prepare(row, carry):
            rows = turn[pl.ds(row, LANES, stride=BAND), :]
            values = rows.T.reshape(tiles, TILE, LANES)
            center = jnp.mean(values, axis=(0, 1), keepdims=True)
            values = values - center
            spread = jnp.mean(values * values, axis=(0, 1), keepdims=True)
            values = values * lax.rsqrt(spread + EPS)
            start[row] = values.astype(jnp.bfloat16).astype(jnp.float32)
            return carry

        lax.fori_loop(0, BAND, prepare, 0)

    def section(level, source, emit):
        half = 1 << level

        def step(i, carry):
            place = i & (half - 1)
            base = (i >> level) * (2 * half)
            low = source[base + place]
            first = source[base + half + place]
            second = source[base + half + jnp.minimum(place + 1, half - 1)]
            row = 2 * i
            for e, high in ((0, first), (1, second)):
                amount = jnp.broadcast_to(table[0, 0, level, pl.ds(row + e, 1), :], (TILE, LANES))[None]
                emit(row + e, low + delay_rows(high, amount))
            return carry

        lax.fori_loop(0, BAND // 2, step, 0)

    def keep(target):
        def emit(row, values):
            target[row] = values
        return emit

    def finish(row, values):
        turn[pl.ds(row, LANES, stride=BAND), :] = (values * scale).reshape(128, LANES).T

    @pl.when(block < counts[0])
    def _():
        section(0, start, keep(ping))
        section(1, ping, keep(pong))
        section(2, pong, keep(ping))
        section(3, ping, keep(pong))
        section(4, pong, finish)
        out[...] = turn[...].astype(jnp.bfloat16).reshape(out.shape)

    @pl.when(block >= counts[0])
    def _():
        out[...] = jnp.zeros_like(out)


def planes(count, raw, table):
    sources = raw.shape[0]
    return pl.pallas_call(
        kernel,
        out_shape=jax.ShapeDtypeStruct((MAXBLK,) + raw.shape, jnp.bfloat16),
        grid_spec=pltpu.PrefetchScalarGridSpec(
            num_scalar_prefetch=1,
            grid=(2, MAXBLK),
            in_specs=[
                pl.BlockSpec((sources, 1, 128, 128), lambda i, j, c: (0, i, 0, 0)),
                pl.BlockSpec((1, 1, SECTIONS, BAND, LANES), lambda i, j, c: (i, j, 0, 0, 0)),
            ],
            out_specs=pl.BlockSpec((1, sources, 1, 128, 128), lambda i, j, c: (j, 0, i, 0, 0)),
            scratch_shapes=[
                pltpu.VMEM((BAND, 16, TILE, LANES), jnp.float32),
                pltpu.VMEM((BAND, 16, TILE, LANES), jnp.float32),
                pltpu.VMEM((BAND, 16, TILE, LANES), jnp.float32),
                pltpu.VMEM((BAND * LANES, LANES), jnp.float32),
            ],
        ),
        compiler_params=pltpu.CompilerParams(vmem_limit_bytes=32 * 2**20),
    )(count, raw, table)


def body(beam_power, trial_blocks, shift_table):
    chan_count = lax.axis_size("chan")
    own = lax.axis_index("grp") * chan_count + lax.axis_index("chan")
    turned = lax.all_to_all(beam_power, "chan", split_axis=0, concat_axis=0, tiled=True)
    raw = turned.reshape(chan_count, 2, 128, 128)
    table = shift_table.reshape(MAXBLK, SECTIONS, chan_count, 2, 4, BAND)
    table = table.transpose(3, 0, 1, 5, 2, 4).reshape(2, MAXBLK, SECTIONS, BAND, LANES)
    count = lax.dynamic_slice(trial_blocks, (own,), (1,))
    return planes(count, raw, table).reshape(1, MAXBLK, -1, 128)


def solution(mesh):
    in_specs = (P("grp", "chan", None), P(), P())
    out_specs = P(("grp", "chan"), None, None, None)
    return jax.shard_map(body, mesh=mesh, in_specs=in_specs, out_specs=out_specs, check_vma=False)
```

```python
import jax
import jax.numpy as jnp
from jax import lax
from jax.experimental import pallas as pl
from jax.experimental.pallas import tpu as pltpu
from jax.sharding import PartitionSpec as P

SECTIONS = 5
MAXBLK = 4
NT = 128
TILE = 8
TILES = NT // TILE
BAND = 32
LANES = 128
PITCH = 40
EPS = 1e-05
SCALE = float(2**SECTIONS) ** (-0.5)


def delayed(rows, tiles):
    pad = jnp.zeros((tiles,) + rows.shape[1:], rows.dtype)
    return jnp.concatenate([pad, rows[:-tiles]], axis=0)


def delay_rows(rows, amount):
    amount = jnp.broadcast_to(amount[None], rows.shape)
    third = amount == 3
    for tiles, chosen in (
        (1, (amount == 1) | third),
        (2, (amount == 2) | third),
        (4, amount == 4),
    ):
        rows = jnp.where(chosen, delayed(rows, tiles), rows)
    return rows


def turned(values):
    row = lax.broadcasted_iota(jnp.int32, (LANES, LANES), 0)
    column = lax.broadcasted_iota(jnp.int32, (LANES, LANES), 1)
    unit = (row == column).astype(jnp.bfloat16)
    return lax.dot_general(unit, values, (((1,), (1,)), ((), ())), preferred_element_type=jnp.float32)


def kernel(counts, raw, table, out, start, ping, pong, lines):
    block = pl.program_id(0)

    def band_row(part, row):
        return pl.ds(part * LANES * PITCH + row, LANES, stride=PITCH)

    @pl.when(block == 0)
    def _():
        def widen(band, carry):
            values = raw[pl.ds(pl.multiple_of(band * BAND, BAND), BAND), :]
            lines[pl.ds(pl.multiple_of(band * PITCH, 8), BAND), :] = values.astype(jnp.float32)
            return carry

        lax.fori_loop(0, 2 * LANES, widen, 0, unroll=8)

        def calibrate(row, carry):
            parts = []
            for part in range(2):
                values = lines[band_row(part, row), :].T.reshape(TILES, TILE, LANES)
                center = jnp.sum(values, axis=(0, 1), keepdims=True) * (1 / NT)
                values = values - center
                spread = jnp.sum(values * values, axis=(0, 1), keepdims=True) * (1 / NT)
                parts.append(values * lax.rsqrt(spread + EPS))
            start[row] = jnp.concatenate(parts, axis=1).astype(jnp.bfloat16)
            return carry

        lax.fori_loop(0, BAND, calibrate, 0, unroll=4)

    def section(level, source, emit, unroll):
        half = 1 << level

        def step(i, carry):
            place = i & (half - 1)
            base = (i >> level) * (2 * half)
            low = source[base + place]
            first = source[base + half + place]
            second = first if half == 1 else source[base + half + jnp.minimum(place + 1, half - 1)]
            for odd, high in ((0, first), (1, second)):
                row = 2 * i + odd
                amount = [jnp.broadcast_to(table[0, level, row, pl.ds(part, 1)], (TILE, LANES)) for part in range(2)]
                emit(row, low, delay_rows(high, jnp.concatenate(amount, axis=0).astype(jnp.bfloat16)))
            return carry

        lax.fori_loop(0, BAND // 2, step, 0, unroll=unroll)

    def keep(target):
        def emit(row, low, high):
            target[row] = low + high

        return emit

    def finish(row, low, high):
        for part in range(2):
            half = slice(part * TILE, (part + 1) * TILE)
            total = low[:, half].astype(jnp.float32) + high[:, half].astype(jnp.float32)
            total = total.reshape(NT, LANES)
            lines[band_row(part, row), :] = turned((total * SCALE).astype(jnp.bfloat16)) if part else total.T

    @pl.when(block < counts[0])
    def _():
        section(0, start, keep(ping), 4)
        section(1, ping, keep(pong), 4)
        section(2, pong, keep(ping), 4)
        section(3, ping, keep(pong), 4)
        section(4, pong, finish, 2)
        for part in range(2):
            def narrow(band, carry):
                values = lines[pl.ds(pl.multiple_of(band * PITCH, 8), BAND), :]
                values = values if part else values * SCALE
                out[0, pl.ds(pl.multiple_of(band * BAND, BAND), BAND), :] = values.astype(jnp.bfloat16)
                return carry

            lax.fori_loop(part * LANES, (part + 1) * LANES, narrow, 0, unroll=8)

    @pl.when(block >= counts[0])
    def _():
        out[...] = jnp.zeros_like(out)


def planes(count, raw, table):
    state = pltpu.VMEM((BAND, TILES, 2 * TILE, LANES), jnp.bfloat16)
    return pl.pallas_call(
        kernel,
        out_shape=jax.ShapeDtypeStruct((MAXBLK,) + raw.shape, jnp.bfloat16),
        grid_spec=pltpu.PrefetchScalarGridSpec(
            num_scalar_prefetch=1,
            grid=(MAXBLK,),
            in_specs=[
                pl.BlockSpec(memory_space=pltpu.VMEM),
                pl.BlockSpec((1, SECTIONS, BAND, 2, LANES), lambda j, c: (j, 0, 0, 0, 0)),
            ],
            out_specs=pl.BlockSpec((1,) + raw.shape, lambda j, c: (j, 0, 0)),
            scratch_shapes=[state, state, state, pltpu.VMEM((2 * LANES * PITCH, LANES), jnp.float32)],
        ),
        compiler_params=pltpu.CompilerParams(vmem_limit_bytes=40 * 2**20),
    )(count, raw, table)


def body(beam_power, trial_blocks, shift_table):
    chan_count = lax.axis_size("chan")
    own = lax.axis_index("grp") * chan_count + lax.axis_index("chan")
    raw = lax.all_to_all(beam_power, "chan", split_axis=0, concat_axis=0, tiled=True).reshape(-1, NT)
    table = shift_table.reshape(MAXBLK, SECTIONS, 2, LANES, BAND).transpose(0, 1, 4, 2, 3).astype(jnp.float32)
    count = lax.dynamic_slice(trial_blocks, (own,), (1,))
    return planes(count, raw, table)[None]


def solution(mesh):
    in_specs = (P("grp", "chan", None), P(), P())
    out_specs = P(("grp", "chan"), None, None, None)
    return jax.shard_map(body, mesh=mesh, in_specs=in_specs, out_specs=out_specs, check_vma=False)
```

```python
import jax
import jax.numpy as jnp
from jax import lax
from jax.experimental import pallas as pl
from jax.experimental.pallas import tpu as pltpu
from jax.sharding import PartitionSpec as P

SECTIONS = 5
MAXBLK = 4
NT = 128
TILE = 8
TILES = NT // TILE
BAND = 32
LANES = 128
BANDS = 2 * LANES
PITCH = 40
EPS = 1e-05
SCALE = float(2**SECTIONS) ** (-0.5)


def delayed(rows, tiles):
    pad = jnp.zeros((tiles,) + rows.shape[1:], rows.dtype)
    return jnp.concatenate([pad, rows[:-tiles]], axis=0)


def delay_rows(rows, amount):
    amount = jnp.broadcast_to(amount[None], rows.shape)
    third = amount == 3
    for tiles, chosen in (
        (1, (amount == 1) | third),
        (2, (amount == 2) | third),
        (4, amount == 4),
    ):
        rows = jnp.where(chosen, delayed(rows, tiles), rows)
    return rows


def kernel(counts, raw, table, out, start, ping, pong, lines, even_held, odd_held):
    block = pl.program_id(0)
    count = counts[0]

    def band_row(part, row):
        return pl.ds(part * LANES * PITCH + row, LANES, stride=PITCH)

    def widen(band, carry):
        values = raw[pl.ds(pl.multiple_of(band * BAND, BAND), BAND), :]
        lines[pl.ds(pl.multiple_of(band * PITCH, 8), BAND), :] = values.astype(jnp.float32)
        return carry

    def narrow(band, carry):
        values = lines[pl.ds(pl.multiple_of(band * PITCH, 8), BAND), :]
        out[0, pl.ds(pl.multiple_of(band * BAND, BAND), BAND), :] = values.astype(jnp.bfloat16)
        return carry

    def calibrate(row, carry):
        parts = []
        for part in range(2):
            values = lines[band_row(part, row), :].T.reshape(TILES, TILE, LANES)
            center = jnp.sum(values, axis=(0, 1), keepdims=True) * (1 / NT)
            values = values - center
            spread = jnp.sum(values * values, axis=(0, 1), keepdims=True) * (1 / NT)
            parts.append(values * lax.rsqrt(spread + EPS))
        start[row] = jnp.concatenate(parts, axis=1).astype(jnp.bfloat16)
        return carry

    def delayed_pair(level, i, first, second):
        for odd, high in ((0, first), (1, second)):
            row = 2 * i + odd
            amount = [jnp.broadcast_to(table[0, level, row, pl.ds(part, 1)], (TILE, LANES)) for part in range(2)]
            yield row, odd, delay_rows(high, jnp.concatenate(amount, axis=0).astype(jnp.bfloat16))

    def section(level, source, target):
        half = 1 << level

        def step(i, carry):
            place = i & (half - 1)
            base = (i >> level) * (2 * half)
            low = source[base + place]
            first = source[base + half + place]
            second = first if half == 1 else source[base + half + jnp.minimum(place + 1, half - 1)]
            for row, _, high in delayed_pair(level, i, first, second):
                target[row] = low + high
            return carry

        lax.fori_loop(0, BAND // 2, step, 0, unroll=8)

    def finish(source):
        half = BAND // 2

        def compute(i, held):
            low = source[i]
            for _, odd, high in delayed_pair(SECTIONS - 1, i, source[half + i], source[half + jnp.minimum(i + 1, half - 1)]):
                for part in range(2):
                    rows = slice(part * TILE, (part + 1) * TILE)
                    total = low[:, rows].astype(jnp.float32) + high[:, rows].astype(jnp.float32)
                    held[part, odd] = (total * SCALE).reshape(NT, LANES)

        def flush(i, held):
            for part in range(2):
                for odd in range(2):
                    lines[band_row(part, 2 * i + odd), :] = held[part, odd].T

        def step(k, carry):
            flush(2 * k, even_held)
            compute(2 * k + 1, odd_held)
            flush(2 * k + 1, odd_held)
            compute(2 * k + 2, even_held)
            return carry

        compute(0, even_held)
        lax.fori_loop(0, half // 2 - 1, step, 0, unroll=True)
        flush(half - 2, even_held)
        compute(half - 1, odd_held)
        flush(half - 1, odd_held)

    @pl.when(block == 0)
    def _():
        lax.fori_loop(0, BANDS, widen, 0, unroll=16)
        lax.fori_loop(0, BAND, calibrate, 0, unroll=16)

    @pl.when(block < count)
    def _():
        section(0, start, ping)
        section(1, ping, pong)
        section(2, pong, ping)
        section(3, ping, pong)
        finish(pong)
        lax.fori_loop(0, BANDS, narrow, 0, unroll=64)

    @pl.when(block >= count)
    def _():
        out[...] = jnp.zeros_like(out)


def planes(count, raw, table):
    state = pltpu.VMEM((BAND, TILES, 2 * TILE, LANES), jnp.bfloat16)
    held = pltpu.VMEM((2, 2, NT, LANES), jnp.float32)
    return pl.pallas_call(
        kernel,
        out_shape=jax.ShapeDtypeStruct((MAXBLK,) + raw.shape, jnp.bfloat16),
        grid_spec=pltpu.PrefetchScalarGridSpec(
            num_scalar_prefetch=1,
            grid=(MAXBLK,),
            in_specs=[
                pl.BlockSpec(memory_space=pltpu.VMEM),
                pl.BlockSpec((1, SECTIONS, BAND, 2, LANES), lambda j, c: (j, 0, 0, 0, 0)),
            ],
            out_specs=pl.BlockSpec((1,) + raw.shape, lambda j, c: (j, 0, 0)),
            scratch_shapes=[state, state, state, pltpu.VMEM((BANDS * PITCH, LANES), jnp.float32), held, held],
        ),
        compiler_params=pltpu.CompilerParams(vmem_limit_bytes=40 * 2**20),
    )(count, raw, table)


def body(beam_power, trial_blocks, shift_table):
    chan_count = lax.axis_size("chan")
    own = lax.axis_index("grp") * chan_count + lax.axis_index("chan")
    raw = lax.all_to_all(beam_power, "chan", split_axis=0, concat_axis=0, tiled=True).reshape(-1, NT)
    table = shift_table.reshape(MAXBLK, SECTIONS, 2, LANES, BAND).transpose(0, 1, 4, 2, 3).astype(jnp.float32)
    count = lax.dynamic_slice(trial_blocks, (own,), (1,))
    return planes(count, raw, table)[None]


def solution(mesh):
    in_specs = (P("grp", "chan", None), P(), P())
    out_specs = P(("grp", "chan"), None, None, None)
    return jax.shard_map(body, mesh=mesh, in_specs=in_specs, out_specs=out_specs, check_vma=False)
```

```python
import jax
import jax.numpy as jnp
from jax import lax
from jax.experimental import pallas as pl
from jax.experimental.pallas import tpu as pltpu
from jax.sharding import PartitionSpec as P

SECTIONS = 5
MAXBLK = 4
NT = 128
TILE = 8
TILES = NT // TILE
BAND = 32
LANES = 128
BANDS = 2 * LANES
PITCH = 33
EPS = 1e-05
SCALE = float(2**SECTIONS) ** (-0.5)


def turned(values):
    row = lax.broadcasted_iota(jnp.int32, (LANES, LANES), 0)
    column = lax.broadcasted_iota(jnp.int32, (LANES, LANES), 1)
    unit = (row == column).astype(jnp.bfloat16)
    return lax.dot_general(unit, values, (((1,), (1,)), ((), ())), preferred_element_type=jnp.float32)


def delayed(rows, tiles):
    pad = jnp.zeros((tiles,) + rows.shape[1:], rows.dtype)
    return jnp.concatenate([pad, rows[:-tiles]], axis=0)


def delay_rows(rows, amount):
    amount = jnp.broadcast_to(amount[None], rows.shape)
    third = amount == 3
    for tiles, chosen in (
        (1, (amount == 1) | third),
        (2, (amount == 2) | third),
        (4, amount == 4),
    ):
        rows = jnp.where(chosen, delayed(rows, tiles), rows)
    return rows


def by_unit(part, odd):
    return part == 1 and odd == 1


def kernel(counts, raw, table, out, start, ping, pong, lines, held_a, held_b, half_a, half_b, rows_a, rows_b):
    block = pl.program_id(0)
    count = counts[0]

    def band_row(part, row):
        return pl.ds(part * LANES * PITCH + row, LANES, stride=PITCH)

    def widen(band, carry):
        values = raw[pl.ds(pl.multiple_of(band * BAND, BAND), BAND), :]
        lines[pl.ds(band * PITCH, BAND), :] = values.astype(jnp.float32)
        return carry

    def fetch(row, held):
        for part in range(2):
            held[part] = lines[band_row(part, row), :].T

    def calibrate(row, held):
        parts = []
        for part in range(2):
            values = held[part].reshape(TILES, TILE, LANES)
            center = jnp.sum(values, axis=(0, 1), keepdims=True) * (1 / NT)
            values = values - center
            spread = jnp.sum(values * values, axis=(0, 1), keepdims=True) * (1 / NT)
            parts.append(values * lax.rsqrt(spread + EPS))
        start[row] = jnp.concatenate(parts, axis=1).astype(jnp.bfloat16)

    def delayed_pair(level, i, first, second):
        for odd, high in ((0, first), (1, second)):
            row = 2 * i + odd
            amount = [jnp.broadcast_to(table[0, level, row, pl.ds(part, 1)], (TILE, LANES)) for part in range(2)]
            yield row, odd, delay_rows(high, jnp.concatenate(amount, axis=0).astype(jnp.bfloat16))

    def section(level, source, target):
        half = 1 << level

        def step(i, carry):
            place = i & (half - 1)
            base = (i >> level) * (2 * half)
            low = source[base + place]
            first = source[base + half + place]
            second = first if half == 1 else source[base + half + jnp.minimum(place + 1, half - 1)]
            for row, _, high in delayed_pair(level, i, first, second):
                target[row] = low + high
            return carry

        lax.fori_loop(0, BAND // 2, step, 0, unroll=8)

    def finish(source):
        half = BAND // 2

        def compute(i, held):
            low = source[i]
            ups = source[half + i], source[half + jnp.minimum(i + 1, half - 1)]
            for _, odd, high in delayed_pair(SECTIONS - 1, i, *ups):
                for part in range(2):
                    rows = slice(part * TILE, (part + 1) * TILE)
                    total = low[:, rows].astype(jnp.float32) + high[:, rows].astype(jnp.float32)
                    if by_unit(part, odd):
                        held[1][...] = (total * SCALE).reshape(NT, LANES).astype(jnp.bfloat16)
                    else:
                        held[0][part, odd] = total.reshape(NT, LANES)

        def flush(i, held):
            for part in range(2):
                for odd in range(2):
                    tile = turned(held[1][...]) if by_unit(part, odd) else held[0][part, odd].T
                    lines[band_row(part, 2 * i + odd), :] = tile

        even, uneven = (held_a, half_a), (held_b, half_b)
        compute(0, even)
        for k in range(half // 2 - 1):
            flush(2 * k, even)
            compute(2 * k + 1, uneven)
            flush(2 * k + 1, uneven)
            compute(2 * k + 2, even)
        flush(half - 2, even)
        compute(half - 1, uneven)
        flush(half - 1, uneven)

    def narrow(part):
        def step(band, carry):
            values = lines[pl.ds(band * PITCH, BAND), :]
            odd = lax.broadcasted_iota(jnp.int32, values.shape, 0) % 2 == 1
            values = values * (jnp.where(odd, 1.0, SCALE) if part else SCALE)
            out[0, pl.ds(pl.multiple_of(band * BAND, BAND), BAND), :] = values.astype(jnp.bfloat16)
            return carry

        lax.fori_loop(part * LANES, (part + 1) * LANES, step, 0, unroll=64)

    @pl.when(block == 0)
    def _():
        lax.fori_loop(0, BANDS, widen, 0, unroll=16)
        fetch(0, rows_a)
        for k in range(BAND // 2 - 1):
            fetch(2 * k + 1, rows_b)
            calibrate(2 * k, rows_a)
            fetch(2 * k + 2, rows_a)
            calibrate(2 * k + 1, rows_b)
        fetch(BAND - 1, rows_b)
        calibrate(BAND - 2, rows_a)
        calibrate(BAND - 1, rows_b)

    @pl.when(block < count)
    def _():
        section(0, start, ping)
        section(1, ping, pong)
        section(2, pong, ping)
        section(3, ping, pong)
        finish(pong)
        narrow(0)
        narrow(1)

    @pl.when(block >= count)
    def _():
        out[...] = jnp.zeros_like(out)


def planes(count, raw, table):
    state = pltpu.VMEM((BAND, TILES, 2 * TILE, LANES), jnp.bfloat16)
    lines = pltpu.VMEM((BANDS * PITCH, LANES), jnp.float32)
    held = pltpu.VMEM((2, 2, NT, LANES), jnp.float32)
    half = pltpu.VMEM((NT, LANES), jnp.bfloat16)
    rows = pltpu.VMEM((2, NT, LANES), jnp.float32)
    return pl.pallas_call(
        kernel,
        out_shape=jax.ShapeDtypeStruct((MAXBLK,) + raw.shape, jnp.bfloat16),
        grid_spec=pltpu.PrefetchScalarGridSpec(
            num_scalar_prefetch=1,
            grid=(MAXBLK,),
            in_specs=[
                pl.BlockSpec(memory_space=pltpu.VMEM),
                pl.BlockSpec((1, SECTIONS, BAND, 2, LANES), lambda j, c: (j, 0, 0, 0, 0)),
            ],
            out_specs=pl.BlockSpec((1,) + raw.shape, lambda j, c: (j, 0, 0)),
            scratch_shapes=[state, state, state, lines, held, held, half, half, rows, rows],
        ),
        compiler_params=pltpu.CompilerParams(vmem_limit_bytes=40 * 2**20),
    )(count, raw, table)


def body(beam_power, trial_blocks, shift_table):
    chan_count = lax.axis_size("chan")
    own = lax.axis_index("grp") * chan_count + lax.axis_index("chan")
    raw = lax.all_to_all(beam_power, "chan", split_axis=0, concat_axis=0, tiled=True).reshape(-1, NT)
    table = shift_table.reshape(MAXBLK, SECTIONS, 2, LANES, BAND).transpose(0, 1, 4, 2, 3).astype(jnp.float32)
    count = lax.dynamic_slice(trial_blocks, (own,), (1,))
    return planes(count, raw, table)[None]


def solution(mesh):
    in_specs = (P("grp", "chan", None), P(), P())
    out_specs = P(("grp", "chan"), None, None, None)
    return jax.shard_map(body, mesh=mesh, in_specs=in_specs, out_specs=out_specs, check_vma=False)
```

```python
import jax
import jax.numpy as jnp
from jax import lax
from jax.experimental import pallas as pl
from jax.experimental.pallas import tpu as pltpu
from jax.sharding import PartitionSpec as P

SECTIONS = 5
MAXBLK = 4
NT = 128
TILE = 8
TILES = NT // TILE
BAND = 32
LANES = 128
BANDS = 2 * LANES
PITCH = 33
EPS = 1e-05
SCALE = float(2**SECTIONS) ** (-0.5)


def turned(values):
    row = lax.broadcasted_iota(jnp.int32, (LANES, LANES), 0)
    column = lax.broadcasted_iota(jnp.int32, (LANES, LANES), 1)
    unit = (row == column).astype(jnp.bfloat16)
    return lax.dot_general(unit, values, (((1,), (1,)), ((), ())), preferred_element_type=jnp.float32)


def delayed(rows, tiles):
    pad = jnp.zeros((tiles,) + rows.shape[1:], rows.dtype)
    return jnp.concatenate([pad, rows[:-tiles]], axis=0)


def delay_rows(rows, amount):
    amount = jnp.broadcast_to(amount[None], rows.shape)
    third = amount == 3
    for tiles, chosen in (
        (1, (amount == 1) | third),
        (2, (amount == 2) | third),
        (4, amount == 4),
    ):
        rows = jnp.where(chosen, delayed(rows, tiles), rows)
    return rows


def by_unit(part, odd):
    return part == 1 and odd == 1


def kernel(counts, raw, table, out, start, ping, pong, lines, held_a, held_b, half_a, half_b, rows_a, rows_b):
    block = pl.program_id(0)
    count = counts[0]

    def band_row(part, row):
        return pl.ds(part * LANES * PITCH + row, LANES, stride=PITCH)

    def widen(band, carry):
        values = raw[pl.ds(pl.multiple_of(band * BAND, BAND), BAND), :]
        lines[pl.ds(band * PITCH, BAND), :] = values.astype(jnp.float32)
        return carry

    def fetch(row, held):
        for part in range(2):
            held[part] = lines[band_row(part, row), :].T

    def calibrate(row, held):
        parts = []
        for part in range(2):
            values = held[part].reshape(TILES, TILE, LANES)
            center = jnp.sum(values, axis=(0, 1), keepdims=True) * (1 / NT)
            values = values - center
            spread = jnp.sum(values * values, axis=(0, 1), keepdims=True) * (1 / NT)
            parts.append(values * lax.rsqrt(spread + EPS))
        start[row] = jnp.concatenate(parts, axis=1).astype(jnp.bfloat16).astype(jnp.float32)

    def delayed_pair(level, i, first, second):
        for odd, high in ((0, first), (1, second)):
            row = 2 * i + odd
            amount = [jnp.broadcast_to(table[0, level, row, pl.ds(part, 1)], (TILE, LANES)) for part in range(2)]
            yield row, odd, delay_rows(high, jnp.concatenate(amount, axis=0))

    def section(level, source, target):
        half = 1 << level

        def step(i, carry):
            place = i & (half - 1)
            base = (i >> level) * (2 * half)
            low = source[base + place]
            first = source[base + half + place]
            second = first if half == 1 else source[base + half + jnp.minimum(place + 1, half - 1)]
            for row, _, high in delayed_pair(level, i, first, second):
                target[row] = low + high
            return carry

        lax.fori_loop(0, BAND // 2, step, 0, unroll=8)

    def finish(source):
        half = BAND // 2

        def compute(i, held):
            low = source[i]
            ups = source[half + i], source[half + jnp.minimum(i + 1, half - 1)]
            for _, odd, high in delayed_pair(SECTIONS - 1, i, *ups):
                for part in range(2):
                    rows = slice(part * TILE, (part + 1) * TILE)
                    total = low[:, rows] + high[:, rows]
                    if by_unit(part, odd):
                        held[1][...] = (total * SCALE).reshape(NT, LANES).astype(jnp.bfloat16)
                    else:
                        held[0][part, odd] = total.reshape(NT, LANES)

        def flush(i, held):
            for part in range(2):
                for odd in range(2):
                    tile = turned(held[1][...]) if by_unit(part, odd) else held[0][part, odd].T
                    lines[band_row(part, 2 * i + odd), :] = tile

        even, uneven = (held_a, half_a), (held_b, half_b)
        compute(0, even)
        for k in range(half // 2 - 1):
            flush(2 * k, even)
            compute(2 * k + 1, uneven)
            flush(2 * k + 1, uneven)
            compute(2 * k + 2, even)
        flush(half - 2, even)
        compute(half - 1, uneven)
        flush(half - 1, uneven)

    def narrow(part):
        def step(band, carry):
            values = lines[pl.ds(band * PITCH, BAND), :]
            odd = lax.broadcasted_iota(jnp.int32, values.shape, 0) % 2 == 1
            values = values * (jnp.where(odd, 1.0, SCALE) if part else SCALE)
            out[0, pl.ds(pl.multiple_of(band * BAND, BAND), BAND), :] = values.astype(jnp.bfloat16)
            return carry

        lax.fori_loop(part * LANES, (part + 1) * LANES, step, 0, unroll=64)

    @pl.when(block == 0)
    def _():
        lax.fori_loop(0, BANDS, widen, 0, unroll=16)
        fetch(0, rows_a)
        for k in range(BAND // 2 - 1):
            fetch(2 * k + 1, rows_b)
            calibrate(2 * k, rows_a)
            fetch(2 * k + 2, rows_a)
            calibrate(2 * k + 1, rows_b)
        fetch(BAND - 1, rows_b)
        calibrate(BAND - 2, rows_a)
        calibrate(BAND - 1, rows_b)

    @pl.when(block < count)
    def _():
        section(0, start, ping)
        section(1, ping, pong)
        section(2, pong, ping)
        section(3, ping, pong)
        finish(pong)
        narrow(0)
        narrow(1)

    @pl.when(block >= count)
    def _():
        out[...] = jnp.zeros_like(out)


def planes(count, raw, table):
    state = pltpu.VMEM((BAND, TILES, 2 * TILE, LANES), jnp.float32)
    lines = pltpu.VMEM((BANDS * PITCH, LANES), jnp.float32)
    held = pltpu.VMEM((2, 2, NT, LANES), jnp.float32)
    half = pltpu.VMEM((NT, LANES), jnp.bfloat16)
    rows = pltpu.VMEM((2, NT, LANES), jnp.float32)
    return pl.pallas_call(
        kernel,
        out_shape=jax.ShapeDtypeStruct((MAXBLK,) + raw.shape, jnp.bfloat16),
        grid_spec=pltpu.PrefetchScalarGridSpec(
            num_scalar_prefetch=1,
            grid=(MAXBLK,),
            in_specs=[
                pl.BlockSpec(memory_space=pltpu.VMEM),
                pl.BlockSpec((1, SECTIONS, BAND, 2, LANES), lambda j, c: (j, 0, 0, 0, 0)),
            ],
            out_specs=pl.BlockSpec((1,) + raw.shape, lambda j, c: (j, 0, 0)),
            scratch_shapes=[state, state, state, lines, held, held, half, half, rows, rows],
        ),
        compiler_params=pltpu.CompilerParams(vmem_limit_bytes=40 * 2**20),
    )(count, raw, table)


def body(beam_power, trial_blocks, shift_table):
    chan_count = lax.axis_size("chan")
    own = lax.axis_index("grp") * chan_count + lax.axis_index("chan")
    raw = lax.all_to_all(beam_power, "chan", split_axis=0, concat_axis=0, tiled=True).reshape(-1, NT)
    table = shift_table.reshape(MAXBLK, SECTIONS, 2, LANES, BAND).transpose(0, 1, 4, 2, 3).astype(jnp.float32)
    count = lax.dynamic_slice(trial_blocks, (own,), (1,))
    return planes(count, raw, table)[None]


def solution(mesh):
    in_specs = (P("grp", "chan", None), P(), P())
    out_specs = P(("grp", "chan"), None, None, None)
    return jax.shard_map(body, mesh=mesh, in_specs=in_specs, out_specs=out_specs, check_vma=False)
```

```python
import jax
import jax.numpy as jnp
from jax import lax
from jax.experimental import pallas as pl
from jax.experimental.pallas import tpu as pltpu
from jax.sharding import PartitionSpec as P

SECTIONS = 5
MAXBLK = 4
NT = 128
TILE = 8
TILES = NT // TILE
BAND = 32
LANES = 128
BANDS = 2 * LANES
PITCH = 33
EPS = 1e-05
SCALE = float(2**SECTIONS) ** (-0.5)


def turned(values):
    row = lax.broadcasted_iota(jnp.int32, (LANES, LANES), 0)
    column = lax.broadcasted_iota(jnp.int32, (LANES, LANES), 1)
    unit = (row == column).astype(jnp.bfloat16)
    return lax.dot_general(unit, values, (((1,), (1,)), ((), ())), preferred_element_type=jnp.float32)


def delayed(rows, tiles):
    pad = jnp.zeros((tiles,) + rows.shape[1:], rows.dtype)
    return jnp.concatenate([pad, rows[:-tiles]], axis=0)


def delay_rows(rows, amount):
    amount = jnp.broadcast_to(amount[None], rows.shape)
    third = amount == 3
    for tiles, chosen in (
        (1, (amount == 1) | third),
        (2, (amount == 2) | third),
        (4, amount == 4),
    ):
        rows = jnp.where(chosen, delayed(rows, tiles), rows)
    return rows


def by_unit(part, odd):
    return part == 1 and odd == 1


def kernel(counts, raw, table, out, start, ping, pong, lines, held_a, held_b, half_a, half_b, rows_a, rows_b):
    block, turn = pl.program_id(0), pl.program_id(1)
    count = counts[0]

    def band_row(part, row):
        return pl.ds(part * LANES * PITCH + row, LANES, stride=PITCH)

    def widen(band, carry):
        values = raw[pl.ds(pl.multiple_of(band * BAND, BAND), BAND), :]
        lines[pl.ds(band * PITCH, BAND), :] = values.astype(jnp.float32)
        return carry

    def fetch(row, held):
        for part in range(2):
            held[part] = lines[band_row(part, row), :].T

    def calibrate(row, held):
        parts = []
        for part in range(2):
            values = held[part].reshape(TILES, TILE, LANES)
            center = jnp.sum(values, axis=(0, 1), keepdims=True) * (1 / NT)
            values = values - center
            spread = jnp.sum(values * values, axis=(0, 1), keepdims=True) * (1 / NT)
            parts.append(values * lax.rsqrt(spread + EPS))
        start[row] = jnp.concatenate(parts, axis=1).astype(jnp.bfloat16).astype(jnp.float32)

    def delayed_pair(level, i, first, second):
        for odd, high in ((0, first), (1, second)):
            row = 2 * i + odd
            amount = [jnp.broadcast_to(table[block, level, row, pl.ds(part, 1)], (TILE, LANES)) for part in range(2)]
            yield row, odd, delay_rows(high, jnp.concatenate(amount, axis=0))

    def section(level, source, target):
        half = 1 << level

        def step(i, carry):
            place = i & (half - 1)
            base = (i >> level) * (2 * half)
            low = source[base + place]
            first = source[base + half + place]
            second = first if half == 1 else source[base + half + jnp.minimum(place + 1, half - 1)]
            for row, _, high in delayed_pair(level, i, first, second):
                target[row] = low + high
            return carry

        lax.fori_loop(0, BAND // 2, step, 0, unroll=8)

    def finish(source):
        half = BAND // 2

        def compute(i, held):
            low = source[i]
            ups = source[half + i], source[half + jnp.minimum(i + 1, half - 1)]
            for _, odd, high in delayed_pair(SECTIONS - 1, i, *ups):
                for part in range(2):
                    rows = slice(part * TILE, (part + 1) * TILE)
                    total = low[:, rows] + high[:, rows]
                    if by_unit(part, odd):
                        held[1][...] = (total * SCALE).reshape(NT, LANES).astype(jnp.bfloat16)
                    else:
                        held[0][part, odd] = total.reshape(NT, LANES)

        def flush(i, held):
            for part in range(2):
                for odd in range(2):
                    tile = turned(held[1][...]) if by_unit(part, odd) else held[0][part, odd].T
                    lines[band_row(part, 2 * i + odd), :] = tile

        even, uneven = (held_a, half_a), (held_b, half_b)
        compute(0, even)
        for k in range(half // 2 - 1):
            flush(2 * k, even)
            compute(2 * k + 1, uneven)
            flush(2 * k + 1, uneven)
            compute(2 * k + 2, even)
        flush(half - 2, even)
        compute(half - 1, uneven)
        flush(half - 1, uneven)

    def narrow(part):
        def step(band, carry):
            values = lines[pl.ds(band * PITCH, BAND), :]
            odd = lax.broadcasted_iota(jnp.int32, values.shape, 0) % 2 == 1
            values = values * (jnp.where(odd, 1.0, SCALE) if part else SCALE)
            out[0, pl.ds(pl.multiple_of((band - part * LANES) * BAND, BAND), BAND), :] = values.astype(jnp.bfloat16)
            return carry

        lax.fori_loop(part * LANES, (part + 1) * LANES, step, 0, unroll=64)

    @pl.when((block == 0) & (turn == 0))
    def _():
        lax.fori_loop(0, BANDS, widen, 0, unroll=16)
        fetch(0, rows_a)
        for k in range(BAND // 2 - 1):
            fetch(2 * k + 1, rows_b)
            calibrate(2 * k, rows_a)
            fetch(2 * k + 2, rows_a)
            calibrate(2 * k + 1, rows_b)
        fetch(BAND - 1, rows_b)
        calibrate(BAND - 2, rows_a)
        calibrate(BAND - 1, rows_b)

    @pl.when((block < count) & (turn == 0))
    def _():
        section(0, start, ping)
        section(1, ping, pong)
        section(2, pong, ping)
        section(3, ping, pong)
        finish(pong)
        narrow(0)

    @pl.when((block < count) & (turn == 1))
    def _():
        narrow(1)

    @pl.when(block >= count)
    def _():
        out[...] = jnp.zeros_like(out)


def planes(count, raw, table):
    state = pltpu.VMEM((BAND, TILES, 2 * TILE, LANES), jnp.float32)
    lines = pltpu.VMEM((BANDS * PITCH, LANES), jnp.float32)
    held = pltpu.VMEM((2, 2, NT, LANES), jnp.float32)
    half = pltpu.VMEM((NT, LANES), jnp.bfloat16)
    rows = pltpu.VMEM((2, NT, LANES), jnp.float32)
    return pl.pallas_call(
        kernel,
        out_shape=jax.ShapeDtypeStruct((MAXBLK,) + raw.shape, jnp.bfloat16),
        grid_spec=pltpu.PrefetchScalarGridSpec(
            num_scalar_prefetch=1,
            grid=(MAXBLK, 2),
            in_specs=[
                pl.BlockSpec(memory_space=pltpu.VMEM),
                pl.BlockSpec(memory_space=pltpu.VMEM),
            ],
            out_specs=pl.BlockSpec((1, raw.shape[0] // 2, NT), lambda j, h, c: (j, h, 0)),
            scratch_shapes=[state, state, state, lines, held, held, half, half, rows, rows],
        ),
        compiler_params=pltpu.CompilerParams(vmem_limit_bytes=40 * 2**20),
    )(count, raw, table)


def body(beam_power, trial_blocks, shift_table):
    chan_count = lax.axis_size("chan")
    own = lax.axis_index("grp") * chan_count + lax.axis_index("chan")
    raw = lax.all_to_all(beam_power, "chan", split_axis=0, concat_axis=0, tiled=True).reshape(-1, NT)
    table = shift_table.reshape(MAXBLK, SECTIONS, 2, LANES, BAND).transpose(0, 1, 4, 2, 3).astype(jnp.float32)
    count = lax.dynamic_slice(trial_blocks, (own,), (1,))
    return planes(count, raw, table)[None]


def solution(mesh):
    in_specs = (P("grp", "chan", None), P(), P())
    out_specs = P(("grp", "chan"), None, None, None)
    return jax.shard_map(body, mesh=mesh, in_specs=in_specs, out_specs=out_specs, check_vma=False)
```
